32 devices in a mesh: row: 8 (over y, x, core), col: 4 (over z).
Axes of the slice: x: 2, y: 2, z: 4, core: 2. Of those that a mesh axis runs over, the one named last changes fastest.
Arguments:
- inputs: bfloat16 [128, 12288], P('col', 'row'), may hold values from -6 to 6
- up_weight: bfloat16 [12288, 24576], P('row', 'col'), may hold values from -0.0546875 to 0.0546875
- down_weight: bfloat16 [24576, 12288], P('col', 'row'), may hold values from -0.078125 to 0.078125
- cotangent: bfloat16 [128, 12288], P('col', 'row'), may hold values from -6 to 6
Outputs:
- outputs: bfloat16 [128, 12288], P('col', 'row')
- input_grad: bfloat16 [128, 12288], P('col', 'row')
- up_grad: bfloat16 [12288, 24576], P('row', 'col')
- down_grad: bfloat16 [24576, 12288], P('col', 'row')
The draws below stay inside these ranges and needn't reach their ends.
All inputs are finite; a program needn't handle non-finite values.
Results may differ from the reference program's by a relative error of at most 0.005.
Values may be sent and summed in bfloat16 or wider, within the bound.
A program may use at most 128 MiB of HBM per device.

```python
import math
import jax
import jax.numpy as jnp
from jax import lax

D = 12288
FF = 24576
TOKENS = 128


def shard_levels(own_key, shape, split, least, top_value):
    loudness = 1.0
    for position, parts in split:
        draws = jax.random.uniform(jax.random.fold_in(jax.random.fold_in(own_key, 6), position), (parts,), jnp.float32, least / len(split), top_value / len(split))
        loudness = loudness * jnp.repeat(jnp.exp(draws), shape[position] // parts).reshape((-1,) + (1,) * (len(shape) - 1 - position))
    return loudness


def scatter_about(stream_key, extent, spread, most, pieces=(), held_as=jnp.bfloat16):
    values = jax.random.normal(stream_key, extent, jnp.float32) * spread
    if len(pieces) > 0:
        values = shard_levels(stream_key, extent, pieces, -0.22, 0.18) * values
    return jnp.clip(values, min=-most, max=most).astype(held_as)


def setup_inputs(seed: int = 0) -> dict:
    arg_keys = jax.random.split(jax.random.key(seed), 5)
    return {
        "inputs": scatter_about(arg_keys[0], (TOKENS, D), 1.0, 6.0, ((0, 4), (1, 8))),
        "up_weight": scatter_about(arg_keys[1], (D, FF), D ** -0.5, 0.0546875, ((0, 8), (1, 4))),
        "down_weight": scatter_about(arg_keys[2], (FF, D), (FF // 4) ** -0.5, 0.078125, ((0, 4), (1, 8))),
        "cotangent": scatter_about(arg_keys[3], (TOKENS, D), 1.0, 6.0, ((0, 4), (1, 8))),
    }


def gelu_value(v):
    cval = math.sqrt(2.0 / math.pi)
    return 0.5 * v * (1.0 + jnp.tanh(cval * (v + 0.044715 * v * v * v)))

def gelu_slope(v):
    cval = math.sqrt(2.0 / math.pi)
    tval = jnp.tanh(cval * (v + 0.044715 * v * v * v))
    return 0.5 * (1.0 + tval) + 0.5 * v * (1.0 - tval * tval) * cval * (1.0 + 3.0 * 0.044715 * v * v)

def reference(inputs, up_weight, down_weight, cotangent):
    preact = jnp.dot(inputs, up_weight, preferred_element_type=jnp.float32)
    activ = gelu_value(preact).astype(jnp.bfloat16)
    outputs = jnp.dot(activ, down_weight, preferred_element_type=jnp.float32).astype(jnp.bfloat16)
    act_grad = lax.dot_general(cotangent, down_weight, (((1,), (1,)), ((), ())), preferred_element_type=jnp.float32)
    pre_grad = (act_grad * gelu_slope(preact)).astype(jnp.bfloat16)
    down_grad = lax.dot_general(activ, cotangent, (((0,), (0,)), ((), ())), preferred_element_type=jnp.float32).astype(jnp.bfloat16)
    up_grad = lax.dot_general(inputs, pre_grad, (((0,), (0,)), ((), ())), preferred_element_type=jnp.float32).astype(jnp.bfloat16)
    input_grad = lax.dot_general(pre_grad, up_weight, (((1,), (1,)), ((), ())), preferred_element_type=jnp.float32).astype(jnp.bfloat16)
    return (outputs, input_grad, up_grad, down_grad)
```

```python
import functools
import math

import jax
import jax.numpy as jnp
from jax import lax
from jax.experimental import pallas as pl
from jax.experimental.pallas import tpu as pltpu
from jax.sharding import PartitionSpec as P

PARTS = 4
BF16 = jnp.bfloat16
F32 = jnp.float32


def gelu_value(v):
    cval = math.sqrt(2.0 / math.pi)
    return 0.5 * v * (1.0 + jnp.tanh(cval * (v + 0.044715 * v * v * v)))


def gelu_slope(v):
    cval = math.sqrt(2.0 / math.pi)
    tval = jnp.tanh(cval * (v + 0.044715 * v * v * v))
    return 0.5 * (1.0 + tval) + 0.5 * v * (1.0 - tval * tval) * cval * (
        1.0 + 3.0 * 0.044715 * v * v
    )


def times(left, right):
    return jnp.dot(left, right, preferred_element_type=F32)


def times_transposed(left, right):
    return lax.dot_general(
        left, right, (((1,), (1,)), ((), ())), preferred_element_type=F32
    )


def over_tokens(left, right):
    return lax.dot_general(
        left, right, (((0,), (0,)), ((), ())), preferred_element_type=F32
    )


def layer_kernel(
    rows, cols,
    x_ref, up_ref, down_ref, cot_ref,
    act_out, pg_out, x_out, cot_out, z_out,
    x_all, cot_all, wu, wd, part, pair_in, pair_sum, chip_in, preact, gathered,
    z_sum, z_low,
    w_sem, zs_sem, zr_sem, ps_sem, pr_sem, cs_sem, cr_sem, gs_sem, gr_sem,
    fs_sem, fr_sem, o_sem, xo_sem,
):
    chips = rows // 2
    tokens, width = x_all.shape
    share = x_ref.shape[0]
    half = tokens // 2
    own = tokens // rows
    cw = wu.shape[2]
    items = 2 * PARTS

    r = lax.axis_index("row")
    z = lax.axis_index("col")
    core = lax.rem(r, 2)
    chip = r // 2
    partner = {"row": r + 1 - 2 * core}

    def peer_chip(k):
        return lax.rem(chip + k, chips)

    def source_chip(k):
        return lax.rem(chip + chips - k, chips)

    def peer(k):
        return {"row": peer_chip(k) * 2 + core}

    def block(side, where):
        return pl.ds(pl.multiple_of(side * half + where * own, 16), own)

    def send(src, dst, s_sem, r_sem, to):
        return pltpu.make_async_remote_copy(
            src_ref=src, dst_ref=dst, send_sem=s_sem, recv_sem=r_sem,
            device_id=to, device_id_type=pl.DeviceIdType.MESH,
        )

    loads = []
    for t in range(2):
        for j in range(PARTS):
            if t == 0:
                cp = pltpu.make_async_copy(
                    up_ref.at[:, pl.ds(j * cw, cw)], wu.at[j], w_sem.at[0, j])
            else:
                cp = pltpu.make_async_copy(
                    down_ref.at[pl.ds(j * cw, cw), :], wd.at[j], w_sem.at[1, j])
            cp.start()
            loads.append(cp)

    barrier = pltpu.get_barrier_semaphore()
    mates = [partner] + [peer(k) for k in range(1, chips)]
    mates += [{"col": lax.rem(z + k, cols)} for k in range(1, cols)]
    for mate in mates:
        pl.semaphore_signal(
            barrier, inc=1, device_id=mate, device_id_type=pl.DeviceIdType.MESH)
    mine = pl.ds(pl.multiple_of(z * share, 16), share)
    x_all[mine, :] = x_ref[...]
    cot_all[mine, :] = cot_ref[...]
    pl.semaphore_wait(barrier, len(mates))

    z_copies = [[], []]
    for t, (ref, whole) in enumerate(((x_ref, x_all), (cot_ref, cot_all))):
        for k in range(1, cols):
            z_copies[t].append(send(
                ref, whole.at[mine, :], zs_sem.at[t, k - 1], zr_sem.at[t, k - 1],
                {"col": lax.rem(z + k, cols)}))
    for cp in z_copies[0]:
        cp.start()
    for cp in z_copies[0]:
        cp.wait_recv()
    for cp in z_copies[1]:
        cp.start()
    out_copies = [pltpu.make_async_copy(x_all, x_out, xo_sem.at[0])]
    out_copies[0].start()

    sent = list(z_copies[0]) + list(z_copies[1])
    pair, chip_copies, gathers, forwards = {}, {}, {}, {}
    tile = cw // 3

    def stage_a(i):
        t, j = divmod(i, PARTS)
        loads[i].wait()
        if t == 0:
            @pl.loop(0, 3)
            def _(n):
                at = pl.ds(pl.multiple_of(n * tile, 128), tile)
                part[i, :, at] = times(x_all[...], wu[j, :, at]).astype(BF16)
        else:
            if j == 0:
                for cp in z_copies[1]:
                    cp.wait_recv()
                out_copies.append(
                    pltpu.make_async_copy(cot_all, cot_out, xo_sem.at[1]))
                out_copies[-1].start()

            @pl.loop(0, 3)
            def _(n):
                at = pl.ds(pl.multiple_of(n * tile, 128), tile)
                part[i, :, at] = times_transposed(
                    cot_all[...], wd[j, at, :]).astype(BF16)
        there = pl.ds(pl.multiple_of((1 - core) * half, 16), half)
        cp = send(part.at[i, there, :], pair_in.at[i], ps_sem.at[i], pr_sem.at[i],
                  partner)
        cp.start()
        pair[i] = cp
        sent.append(cp)

    def pair_total(i, where):
        low = pl.ds(pl.multiple_of(where * own, 16), own)
        return (part[i, block(core, where), :].astype(F32)
                + pair_in[i, low, :].astype(F32))

    def stage_b(i):
        pair[i].wait_recv()
        chip_copies[i] = []
        for k in range(1, chips):
            pair_sum[i, k - 1, :, :] = pair_total(i, peer_chip(k)).astype(BF16)
            cp = send(pair_sum.at[i, k - 1], chip_in.at[i, k - 1],
                      cs_sem.at[i, k - 1], cr_sem.at[i, k - 1], peer(k))
            cp.start()
            chip_copies[i].append(cp)
            sent.append(cp)

    def stage_c(i):
        t, j = divmod(i, PARTS)
        total = pair_total(i, chip)
        for k in range(1, chips):
            chip_copies[i][k - 1].wait_recv()
            total = total + chip_in[i, k - 1, :, :].astype(F32)
        here = block(core, chip)
        if t == 0:
            preact[j, :, :] = total
            gathered[i, here, :] = gelu_value(total).astype(BF16)
        else:
            gathered[i, here, :] = (total * gelu_slope(preact[j, :, :])).astype(BF16)
        gathers[i], forwards[i] = [], []
        mine_ref = gathered.at[i, here, :]
        for k in range(1, chips):
            cp = send(mine_ref, mine_ref, gs_sem.at[i, k - 1], gr_sem.at[i, k - 1],
                      peer(k))
            cp.start()
            gathers[i].append(cp)
            sent.append(cp)
        cp = send(mine_ref, mine_ref, fs_sem.at[i, 0], fr_sem.at[i, 0], partner)
        cp.start()
        forwards[i].append(cp)
        sent.append(cp)

    def stage_d(i):
        for k in range(1, chips):
            gathers[i][k - 1].wait_recv()
            ref = gathered.at[i, block(core, source_chip(k)), :]
            cp = send(ref, ref, fs_sem.at[i, k], fr_sem.at[i, k], partner)
            cp.start()
            forwards[i].append(cp)
            sent.append(cp)

    wtile = width // 3

    def stage_e(i):
        t, j = divmod(i, PARTS)
        for cp in forwards[i]:
            cp.wait_recv()
        target = act_out if t == 0 else pg_out
        cp = pltpu.make_async_copy(
            gathered.at[i], target.at[:, pl.ds(j * cw, cw)], o_sem.at[i])
        cp.start()
        out_copies.append(cp)

        @pl.loop(0, 3)
        def _(n):
            at = pl.ds(pl.multiple_of(n * wtile, 128), wtile)
            if t == 0:
                term = times(gathered[i], wd[j, :, at])
            else:
                term = times_transposed(gathered[i], wu[j, at, :])
            if j > 0:
                term = term + z_sum[t, :, at]
            if j < PARTS - 1:
                z_sum[t, :, at] = term
            else:
                z_low[t, :, at] = term.astype(BF16)

        if j == PARTS - 1:
            cp = pltpu.make_async_copy(z_low.at[t], z_out.at[t], xo_sem.at[2 + t])
            cp.start()
            out_copies.append(cp)

    stages = (stage_a, stage_b, stage_c, stage_d, stage_e)
    for step in range(items + len(stages) - 1):
        for lag, stage in enumerate(stages):
            if 0 <= step - lag < items:
                stage(step - lag)

    for cp in sent:
        cp.wait_send()
    for cp in out_copies:
        cp.wait()


def per_device(rows, cols, inputs, up_weight, down_weight, cotangent):
    share, width = inputs.shape
    hidden = up_weight.shape[1]
    tokens = share * cols
    chips = rows // 2
    items = 2 * PARTS
    cw = hidden // PARTS
    own = tokens // rows
    dma = pltpu.SemaphoreType.DMA
    anywhere = pl.BlockSpec(memory_space=pl.ANY)
    in_vmem = pl.BlockSpec(memory_space=pltpu.VMEM)

    activ, pregrad, all_inputs, all_cotangent, partial = pl.pallas_call(
        functools.partial(layer_kernel, rows, cols),
        out_shape=(
            jax.ShapeDtypeStruct((tokens, hidden), BF16),
            jax.ShapeDtypeStruct((tokens, hidden), BF16),
            jax.ShapeDtypeStruct((tokens, width), BF16),
            jax.ShapeDtypeStruct((tokens, width), BF16),
            jax.ShapeDtypeStruct((2, tokens, width), BF16),
        ),
        in_specs=[in_vmem, anywhere, anywhere, in_vmem],
        out_specs=(anywhere,) * 5,
        scratch_shapes=[
            pltpu.VMEM((tokens, width), BF16),
            pltpu.VMEM((tokens, width), BF16),
            pltpu.VMEM((PARTS, width, cw), BF16),
            pltpu.VMEM((PARTS, cw, width), BF16),
            pltpu.VMEM((items, tokens, cw), BF16),
            pltpu.VMEM((items, tokens // 2, cw), BF16),
            pltpu.VMEM((items, chips - 1, own, cw), BF16),
            pltpu.VMEM((items, chips - 1, own, cw), BF16),
            pltpu.VMEM((PARTS, own, cw), F32),
            pltpu.VMEM((items, tokens, cw), BF16),
            pltpu.VMEM((2, tokens, width), F32),
            pltpu.VMEM((2, tokens, width), BF16),
            dma((2, PARTS)),
            dma((2, cols - 1)),
            dma((2, cols - 1)),
            dma((items,)),
            dma((items,)),
            dma((items, chips - 1)),
            dma((items, chips - 1)),
            dma((items, chips - 1)),
            dma((items, chips - 1)),
            dma((items, chips)),
            dma((items, chips)),
            dma((items,)),
            dma((4,)),
        ],
        compiler_params=pltpu.CompilerParams(
            collective_id=0, has_side_effects=True, vmem_limit_bytes=58 * 2**20),
        cost_estimate=pl.CostEstimate(
            flops=8 * tokens * width * hidden,
            bytes_accessed=4 * width * hidden,
            transcendentals=2 * own * hidden),
    )(inputs, up_weight, down_weight, cotangent)

    me = lax.axis_index("col")

    def piece(k):
        start = lax.rem(me + k, cols) * share
        return lax.dynamic_slice_in_dim(partial, start, share, axis=1)

    arrived = [
        lax.ppermute(piece(k), "col", [(s, (s + k) % cols) for s in range(cols)])
        for k in range(1, cols)
    ]
    down_grad = over_tokens(activ, all_cotangent).astype(BF16)
    up_grad = over_tokens(all_inputs, pregrad).astype(BF16)
    total = piece(0).astype(F32)
    for other in arrived:
        total = total + other.astype(F32)
    total = total.astype(BF16)
    return (total[0], total[1], up_grad, down_grad)


def solution(mesh):
    placed = (P("col", "row"), P("row", "col"), P("col", "row"), P("col", "row"))
    return jax.shard_map(
        functools.partial(per_device, mesh.shape["row"], mesh.shape["col"]),
        mesh=mesh,
        in_specs=placed,
        out_specs=(P("col", "row"), P("col", "row"), P("row", "col"), P("col", "row")),
        check_vma=False,
    )
```

```python
import functools
import math

import jax
import jax.numpy as jnp
from jax import lax
from jax.experimental import pallas as pl
from jax.experimental.pallas import tpu as pltpu
from jax.sharding import PartitionSpec as P

PARTS = 4
BF16 = jnp.bfloat16
F32 = jnp.float32


def gelu_value(v):
    cval = math.sqrt(2.0 / math.pi)
    return 0.5 * v * (1.0 + jnp.tanh(cval * (v + 0.044715 * v * v * v)))


def gelu_slope(v):
    cval = math.sqrt(2.0 / math.pi)
    tval = jnp.tanh(cval * (v + 0.044715 * v * v * v))
    return 0.5 * (1.0 + tval) + 0.5 * v * (1.0 - tval * tval) * cval * (
        1.0 + 3.0 * 0.044715 * v * v
    )


def times(left, right):
    return jnp.dot(left, right, preferred_element_type=F32)


def times_transposed(left, right):
    return lax.dot_general(
        left, right, (((1,), (1,)), ((), ())), preferred_element_type=F32
    )


def over_tokens(left, right):
    return lax.dot_general(
        left, right, (((0,), (0,)), ((), ())), preferred_element_type=F32
    )


def layer_kernel(
    rows, cols,
    x_ref, up_ref, down_ref, cot_ref,
    act_out, pg_out, x_out, cot_out, *rest,
):
    z_outs = rest[:cols]
    (x_all, cot_all, wu, wd, part, pair_in, pair_sum, chip_in, preact, gathered,
    z_sum, z_low,
    w_sem, zs_sem, zr_sem, ps_sem, pr_sem, cs_sem, cr_sem, gs_sem, gr_sem,
    fs_sem, fr_sem, o_sem, xo_sem, zo_sem) = rest[cols:]
    chips = rows // 2
    tokens, width = x_all.shape
    share = x_ref.shape[0]
    half = tokens // 2
    own = tokens // rows
    cw = wu.shape[2]
    items = 2 * PARTS

    r = lax.axis_index("row")
    z = lax.axis_index("col")
    core = lax.rem(r, 2)
    chip = r // 2
    partner = {"row": r + 1 - 2 * core}

    def peer_chip(k):
        return lax.rem(chip + k, chips)

    def source_chip(k):
        return lax.rem(chip + chips - k, chips)

    def peer(k):
        return {"row": peer_chip(k) * 2 + core}

    def block(side, where):
        return pl.ds(pl.multiple_of(side * half + where * own, 16), own)

    def send(src, dst, s_sem, r_sem, to):
        return pltpu.make_async_remote_copy(
            src_ref=src, dst_ref=dst, send_sem=s_sem, recv_sem=r_sem,
            device_id=to, device_id_type=pl.DeviceIdType.MESH,
        )

    loads = []
    for t in range(2):
        for j in range(PARTS):
            if t == 0:
                cp = pltpu.make_async_copy(
                    up_ref.at[:, pl.ds(j * cw, cw)], wu.at[j], w_sem.at[0, j])
            else:
                cp = pltpu.make_async_copy(
                    down_ref.at[pl.ds(j * cw, cw), :], wd.at[j], w_sem.at[1, j])
            cp.start()
            loads.append(cp)

    barrier = pltpu.get_barrier_semaphore()
    mates = [partner] + [peer(k) for k in range(1, chips)]
    mates += [{"col": lax.rem(z + k, cols)} for k in range(1, cols)]
    for mate in mates:
        pl.semaphore_signal(
            barrier, inc=1, device_id=mate, device_id_type=pl.DeviceIdType.MESH)
    mine = pl.ds(pl.multiple_of(z * share, 16), share)
    x_all[mine, :] = x_ref[...]
    cot_all[mine, :] = cot_ref[...]
    pl.semaphore_wait(barrier, len(mates))

    z_copies = [[], []]
    for t, (ref, whole) in enumerate(((x_ref, x_all), (cot_ref, cot_all))):
        for k in range(1, cols):
            z_copies[t].append(send(
                ref, whole.at[mine, :], zs_sem.at[t, k - 1], zr_sem.at[t, k - 1],
                {"col": lax.rem(z + k, cols)}))
    for cp in z_copies[0]:
        cp.start()
    for cp in z_copies[0]:
        cp.wait_recv()
    for cp in z_copies[1]:
        cp.start()
    out_copies = [pltpu.make_async_copy(x_all, x_out, xo_sem.at[0])]
    out_copies[0].start()

    sent = list(z_copies[0]) + list(z_copies[1])
    pair, chip_copies, gathers, forwards = {}, {}, {}, {}
    tile = cw // 3

    def stage_a(i):
        t, j = divmod(i, PARTS)
        loads[i].wait()
        if t == 0:
            @pl.loop(0, 3)
            def _(n):
                at = pl.ds(pl.multiple_of(n * tile, 128), tile)
                part[i, :, at] = times(x_all[...], wu[j, :, at])
        else:
            if j == 0:
                for cp in z_copies[1]:
                    cp.wait_recv()
                out_copies.append(
                    pltpu.make_async_copy(cot_all, cot_out, xo_sem.at[1]))
                out_copies[-1].start()

            @pl.loop(0, 3)
            def _(n):
                at = pl.ds(pl.multiple_of(n * tile, 128), tile)
                part[i, :, at] = times_transposed(cot_all[...], wd[j, at, :])
        there = pl.ds(pl.multiple_of((1 - core) * half, 16), half)
        cp = send(part.at[i, there, :], pair_in.at[i], ps_sem.at[i], pr_sem.at[i],
                  partner)
        cp.start()
        pair[i] = cp
        sent.append(cp)

    def pair_total(i, where):
        low = pl.ds(pl.multiple_of(where * own, 16), own)
        return part[i, block(core, where), :] + pair_in[i, low, :]

    def stage_b(i):
        pair[i].wait_recv()
        chip_copies[i] = []
        for k in range(1, chips):
            pair_sum[i, k - 1, :, :] = pair_total(i, peer_chip(k)).astype(BF16)
            cp = send(pair_sum.at[i, k - 1], chip_in.at[i, k - 1],
                      cs_sem.at[i, k - 1], cr_sem.at[i, k - 1], peer(k))
            cp.start()
            chip_copies[i].append(cp)
            sent.append(cp)

    def stage_c(i):
        t, j = divmod(i, PARTS)
        total = pair_total(i, chip)
        for k in range(1, chips):
            chip_copies[i][k - 1].wait_recv()
            total = total + chip_in[i, k - 1, :, :].astype(F32)
        here = block(core, chip)
        if t == 0:
            preact[j, :, :] = total
            gathered[i, here, :] = gelu_value(total).astype(BF16)
        else:
            gathered[i, here, :] = (total * gelu_slope(preact[j, :, :])).astype(BF16)
        gathers[i], forwards[i] = [], []
        mine_ref = gathered.at[i, here, :]
        for k in range(1, chips):
            cp = send(mine_ref, mine_ref, gs_sem.at[i, k - 1], gr_sem.at[i, k - 1],
                      peer(k))
            cp.start()
            gathers[i].append(cp)
            sent.append(cp)
        cp = send(mine_ref, mine_ref, fs_sem.at[i, 0], fr_sem.at[i, 0], partner)
        cp.start()
        forwards[i].append(cp)
        sent.append(cp)

    def stage_d(i):
        for k in range(1, chips):
            gathers[i][k - 1].wait_recv()
            ref = gathered.at[i, block(core, source_chip(k)), :]
            cp = send(ref, ref, fs_sem.at[i, k], fr_sem.at[i, k], partner)
            cp.start()
            forwards[i].append(cp)
            sent.append(cp)

    wtile = width // 3

    def stage_e(i):
        t, j = divmod(i, PARTS)
        for cp in forwards[i]:
            cp.wait_recv()
        target = act_out if t == 0 else pg_out
        cp = pltpu.make_async_copy(
            gathered.at[i], target.at[:, pl.ds(j * cw, cw)], o_sem.at[i])
        cp.start()
        out_copies.append(cp)

        @pl.loop(0, 3)
        def _(n):
            at = pl.ds(pl.multiple_of(n * wtile, 128), wtile)
            if t == 0:
                term = times(gathered[i], wd[j, :, at])
            else:
                term = times_transposed(gathered[i], wu[j, at, :])
            if j > 0:
                term = term + z_sum[t, :, at]
            if j < PARTS - 1:
                z_sum[t, :, at] = term
            else:
                z_low[t, :, at] = term.astype(BF16)

        if j == PARTS - 1:
            for k in range(cols):
                rows_k = pl.ds(
                    pl.multiple_of(lax.rem(z + k, cols) * share, 16), share)
                cp = pltpu.make_async_copy(
                    z_low.at[t, rows_k, :], z_outs[k].at[t], zo_sem.at[t, k])
                cp.start()
                out_copies.append(cp)

    stages = (stage_a, stage_b, stage_c, stage_d, stage_e)
    for step in range(items + len(stages) - 1):
        for lag, stage in enumerate(stages):
            if 0 <= step - lag < items:
                stage(step - lag)

    for cp in sent:
        cp.wait_send()
    for cp in out_copies:
        cp.wait()


def grads_kernel(x_ref, cot_ref, act_ref, pg_ref, up_out, down_out, x_turned):
    @pl.when(pl.program_id(0) == 0)
    def _():
        x_turned[...] = x_ref[...].T

    width = x_ref.shape[1]
    rows_at_once = width // 6
    for n in range(6):
        at = pl.ds(n * rows_at_once, rows_at_once)
        up_out[at, :] = times(x_turned[at, :], pg_ref[...]).astype(BF16)
    acts = act_ref[...].T
    down_cols = width // 3
    for n in range(3):
        at = pl.ds(n * down_cols, down_cols)
        down_out[:, at] = times(acts, cot_ref[:, at]).astype(BF16)


def weight_grads(inputs, cotangent, activ, pregrad):
    tokens, width = inputs.shape
    hidden = activ.shape[1]
    steps = width // 128
    span = hidden // steps
    fixed = pl.BlockSpec((tokens, width), lambda i: (0, 0))
    moving = pl.BlockSpec((tokens, span), lambda i: (0, i))
    return pl.pallas_call(
        grads_kernel,
        grid=(steps,),
        out_shape=(
            jax.ShapeDtypeStruct((width, hidden), BF16),
            jax.ShapeDtypeStruct((hidden, width), BF16),
        ),
        in_specs=[fixed, fixed, moving, moving],
        out_specs=(
            pl.BlockSpec((width, span), lambda i: (0, i)),
            pl.BlockSpec((span, width), lambda i: (i, 0)),
        ),
        scratch_shapes=[pltpu.VMEM((width, tokens), BF16)],
        compiler_params=pltpu.CompilerParams(vmem_limit_bytes=32 * 2**20),
        cost_estimate=pl.CostEstimate(
            flops=4 * tokens * width * hidden,
            bytes_accessed=4 * width * hidden,
            transcendentals=0),
    )(inputs, cotangent, activ, pregrad)


def per_device(rows, cols, inputs, up_weight, down_weight, cotangent):
    share, width = inputs.shape
    hidden = up_weight.shape[1]
    tokens = share * cols
    chips = rows // 2
    items = 2 * PARTS
    cw = hidden // PARTS
    own = tokens // rows
    dma = pltpu.SemaphoreType.DMA
    anywhere = pl.BlockSpec(memory_space=pl.ANY)
    in_vmem = pl.BlockSpec(memory_space=pltpu.VMEM)

    activ, pregrad, all_inputs, all_cotangent, *pieces = pl.pallas_call(
        functools.partial(layer_kernel, rows, cols),
        out_shape=(
            jax.ShapeDtypeStruct((tokens, hidden), BF16),
            jax.ShapeDtypeStruct((tokens, hidden), BF16),
            jax.ShapeDtypeStruct((tokens, width), BF16),
            jax.ShapeDtypeStruct((tokens, width), BF16),
        ) + (jax.ShapeDtypeStruct((2, share, width), BF16),) * cols,
        in_specs=[in_vmem, anywhere, anywhere, in_vmem],
        out_specs=(anywhere,) * (4 + cols),
        scratch_shapes=[
            pltpu.VMEM((tokens, width), BF16),
            pltpu.VMEM((tokens, width), BF16),
            pltpu.VMEM((PARTS, width, cw), BF16),
            pltpu.VMEM((PARTS, cw, width), BF16),
            pltpu.VMEM((items, tokens, cw), F32),
            pltpu.VMEM((items, tokens // 2, cw), F32),
            pltpu.VMEM((items, chips - 1, own, cw), BF16),
            pltpu.VMEM((items, chips - 1, own, cw), BF16),
            pltpu.VMEM((PARTS, own, cw), F32),
            pltpu.VMEM((items, tokens, cw), BF16),
            pltpu.VMEM((2, tokens, width), F32),
            pltpu.VMEM((2, tokens, width), BF16),
            dma((2, PARTS)),
            dma((2, cols - 1)),
            dma((2, cols - 1)),
            dma((items,)),
            dma((items,)),
            dma((items, chips - 1)),
            dma((items, chips - 1)),
            dma((items, chips - 1)),
            dma((items, chips - 1)),
            dma((items, chips)),
            dma((items, chips)),
            dma((items,)),
            dma((2,)),
            dma((2, cols)),
        ],
        compiler_params=pltpu.CompilerParams(
            collective_id=0, has_side_effects=True, vmem_limit_bytes=58 * 2**20),
        cost_estimate=pl.CostEstimate(
            flops=8 * tokens * width * hidden,
            bytes_accessed=4 * width * hidden,
            transcendentals=2 * own * hidden),
    )(inputs, up_weight, down_weight, cotangent)

    arrived = [
        lax.ppermute(pieces[k], "col", [(s, (s + k) % cols) for s in range(cols)])
        for k in range(1, cols)
    ]
    up_grad, down_grad = weight_grads(all_inputs, all_cotangent, activ, pregrad)

    def total(t):
        terms = pieces[0][t].astype(F32)
        for other in arrived:
            terms = terms + other[t].astype(F32)
        return terms.astype(BF16)

    return (total(0), total(1), up_grad, down_grad)


def solution(mesh):
    placed = (P("col", "row"), P("row", "col"), P("col", "row"), P("col", "row"))
    return jax.shard_map(
        functools.partial(per_device, mesh.shape["row"], mesh.shape["col"]),
        mesh=mesh,
        in_specs=placed,
        out_specs=(P("col", "row"), P("col", "row"), P("row", "col"), P("col", "row")),
        check_vma=False,
    )
```
